128 devices in a mesh: section: 2 (over core), ctx: 16 (over x, y), fsdp: 4 (over z).
Axes of the slice: x: 4, y: 4, z: 4, core: 2. Of those that a mesh axis runs over, the one named last changes fastest.
Arguments:
- inputs: bfloat16 [4, 4, 1024, 576], P(None, 'fsdp', 'ctx'), may hold values from -6 to 6
- piece_order: int32 [4, 4, 32], P(None, 'fsdp'), may hold values from 0 to 31, as said below
- cotangent: bfloat16 [4, 4, 1024, 576], P(None, 'fsdp', 'ctx'), may hold values from -6 to 6
- gain_attn: bfloat16 [2, 576], P('section', 'fsdp'), may hold values from 0.5 to 1.5
- w_query: bfloat16 [2, 576, 576], P('section', 'fsdp'), may hold values from -0.25 to 0.25
- key_weight: bfloat16 [2, 576, 192], P('section', 'fsdp'), may hold values from -0.25 to 0.25
- value_weight: bfloat16 [2, 576, 192], P('section', 'fsdp'), may hold values from -0.25 to 0.25
- w_out: bfloat16 [2, 576, 576], P('section', None, 'fsdp'), may hold values from -4 to 4
- gain_mlp: bfloat16 [2, 576], P('section', 'fsdp'), may hold values from 0.5 to 1.5
- w_gate: bfloat16 [2, 576, 1536], P('section', 'fsdp'), may hold values from -0.25 to 0.25
- w_up: bfloat16 [2, 576, 1536], P('section', 'fsdp'), may hold values from -0.25 to 0.25
- w_down: bfloat16 [2, 1536, 576], P('section', None, 'fsdp'), may hold values from -0.15625 to 0.15625
Outputs:
- acts: bfloat16 [2, 4, 4, 1024, 576], P('section', None, 'fsdp', 'ctx')
- input_grads: bfloat16 [2, 4, 4, 1024, 576], P('section', None, 'fsdp', 'ctx')
- grad_gain_attn: float32 [2, 576], P('section', 'fsdp')
- grad_query: float32 [2, 576, 576], P('section', 'fsdp')
- grad_key: float32 [2, 576, 192], P('section', 'fsdp')
- grad_value: float32 [2, 576, 192], P('section', 'fsdp')
- grad_out: float32 [2, 576, 576], P('section', None, 'fsdp')
- grad_gain_mlp: float32 [2, 576], P('section', 'fsdp')
- grad_gate: float32 [2, 576, 1536], P('section', 'fsdp')
- grad_up: float32 [2, 576, 1536], P('section', 'fsdp')
- grad_down: float32 [2, 1536, 576], P('section', None, 'fsdp')
The draws below stay inside these ranges and needn't reach their ends.
Inputs may be any that keep to these rules, and one draw needn't show every extreme that they name: `piece_order`: along the last dimension every number appears once, and entries 2c and 2c + 1 hold a pair j and 31 - j.
All inputs are finite; a program needn't handle non-finite values.
Results may differ from the reference program's by a relative error of at most 0.039.
Values may be sent and summed in bfloat16 or wider, within the bound.
A program may use at most 192 MiB of HBM per device.

```python
import math
import jax
import jax.numpy as jnp
from jax import lax

MODEL_DIMENSION = 576
QUERY_HEADS = 9
KEY_VALUE_HEADS = 3
HEAD_SIZE = 64
FF = 1536
MICRO = 4
PIECE = 32
SEQUENCE_TOKENS = 1024
SEQS = 4


def draw_piece_order(key, part):
    key = jax.random.fold_in(key, 11)
    pair_count = SEQUENCE_TOKENS // (2 * PIECE)
    seq_total = MICRO * SEQS
    perm_key, flip_key = jax.random.split(key)
    scores = jax.random.randint(perm_key, (seq_total, pair_count), 0, 1 << 20) * pair_count + jnp.arange(pair_count, dtype=jnp.int32)[None, :]
    ranked = jnp.argsort(scores, axis=-1, stable=True).astype(jnp.int32)
    flip_bits = jax.random.randint(flip_key, (seq_total, pair_count), 0, 2)
    mirror = 2 * pair_count - 1 - ranked
    leading = jnp.where(flip_bits == 1, mirror, ranked)
    trailing = jnp.where(flip_bits == 1, ranked, mirror)
    return jnp.stack([leading, trailing], axis=-1).reshape(MICRO, SEQS, 2 * pair_count).astype(jnp.int32)


def steps_of(key, dims, cuts, least, high):
    factor_of = 1.0
    for position, shards_of in cuts:
        draws = jax.random.uniform(jax.random.fold_in(jax.random.fold_in(key, 6), position), (shards_of,), jnp.float32, least / len(cuts), high / len(cuts))
        factor_of = factor_of * jnp.repeat(jnp.exp(draws), dims[position] // shards_of).reshape((-1,) + (1,) * (len(dims) - 1 - position))
    return factor_of


def noise(rng, shape, width, bound, pieces=(), held_as=jnp.bfloat16):
    level = steps_of(rng, shape, pieces, -0.22, 0.18) if pieces else 1.0
    result = jax.random.normal(rng, shape, jnp.float32) * width * level
    return jnp.minimum(jnp.maximum(result, -bound), bound).astype(held_as)


def setup_inputs(seed: int = 0) -> dict:
    splits = jax.random.split(jax.random.key(seed), 13)
    inputs = noise(splits[0], (MICRO, SEQS, SEQUENCE_TOKENS, MODEL_DIMENSION), 1.0, 6.0, ((1, 4), (2, 16)))
    piece_order = draw_piece_order(jax.random.fold_in(splits[12], 71), 0)
    cotangent = noise(splits[2], (MICRO, SEQS, SEQUENCE_TOKENS, MODEL_DIMENSION), 1.0, 6.0, ((1, 4), (2, 16)))
    gain_attn = jnp.clip(1.0 + 0.1 * jax.random.normal(splits[3], (2, MODEL_DIMENSION), jnp.float32), 0.5, 1.5).astype(jnp.bfloat16)
    w_query = noise(splits[4], (2, MODEL_DIMENSION, QUERY_HEADS * HEAD_SIZE), MODEL_DIMENSION ** -0.5, 0.25, ((0, 2), (1, 4)))
    key_weight = noise(splits[5], (2, MODEL_DIMENSION, KEY_VALUE_HEADS * HEAD_SIZE), MODEL_DIMENSION ** -0.5, 0.25, ((0, 2), (1, 4)))
    value_weight = noise(splits[6], (2, MODEL_DIMENSION, KEY_VALUE_HEADS * HEAD_SIZE), MODEL_DIMENSION ** -0.5, 0.25, ((0, 2), (1, 4)))
    w_out = noise(splits[7], (2, QUERY_HEADS * HEAD_SIZE, MODEL_DIMENSION), (max(1, QUERY_HEADS * HEAD_SIZE // 256)) ** -0.5, 4.0, ((0, 2), (2, 4)))
    gain_mlp = jnp.clip(1.0 + 0.1 * jax.random.normal(splits[8], (2, MODEL_DIMENSION), jnp.float32), 0.5, 1.5).astype(jnp.bfloat16)
    w_gate = noise(splits[9], (2, MODEL_DIMENSION, FF), MODEL_DIMENSION ** -0.5, 0.25, ((0, 2), (1, 4)))
    w_up = noise(splits[10], (2, MODEL_DIMENSION, FF), MODEL_DIMENSION ** -0.5, 0.25, ((0, 2), (1, 4)))
    w_down = noise(splits[11], (2, FF, MODEL_DIMENSION), FF ** -0.5, 0.15625, ((0, 2), (2, 4)))
    return dict(inputs=inputs, piece_order=piece_order, cotangent=cotangent, gain_attn=gain_attn, w_query=w_query, key_weight=key_weight, value_weight=value_weight, w_out=w_out, gain_mlp=gain_mlp, w_gate=w_gate, w_up=w_up, w_down=w_down)


eps_norm = 1e-05
rope_base = 100000.0
negative_filler = -1e+30

@jax.custom_vjp
def reduced_input(v):
    return lax.optimization_barrier(v.astype(jnp.bfloat16)).astype(jnp.float32)

@jax.custom_vjp
def reduced_backward(v):
    return v

def low_keep(v):
    return (reduced_input(v), None)

def low_pass(kept, grad):
    return (grad,)

def back_keep(v):
    return (v, None)

def back_low(kept, grad):
    return (reduced_input(grad),)
reduced_input.defvjp(low_keep, low_pass)
reduced_backward.defvjp(back_keep, back_low)

def matrix_product_exact(first_op, second_op):
    return jnp.dot(first_op, second_op, precision=lax.Precision.HIGHEST, preferred_element_type=jnp.float32)

def rms_norm(values, gain_vec):
    return values * lax.rsqrt(lax.optimization_barrier(jnp.mean(values * values, axis=-1, keepdims=True)) + eps_norm) * gain_vec

def rotary_embed(values, token_positions):
    half_dim = values.shape[-1] // 2
    frequency = rope_base ** (-jnp.arange(half_dim, dtype=jnp.float32) / half_dim)
    angles = token_positions.astype(jnp.float32)[:, None] * frequency[None, :]
    cosine = jnp.cos(angles)[:, None, :]
    sine_part = jnp.sin(angles)[:, None, :]
    first_half = values[..., :half_dim]
    second_half = values[..., half_dim:]
    return jnp.concatenate([first_half * cosine - second_half * sine_part, second_half * cosine + first_half * sine_part], axis=-1)

def attend_block(query_rows, key_head_rows, value_head_rows, query_pos, key_pos):
    local_rows = query_rows.shape[0]
    grouped_heads = query_rows.reshape(local_rows, KEY_VALUE_HEADS, QUERY_HEADS // KEY_VALUE_HEADS, HEAD_SIZE)
    scores = jnp.einsum('qkgd,skd->qkgs', grouped_heads, key_head_rows, precision=lax.Precision.HIGHEST) * (1.0 / math.sqrt(HEAD_SIZE))
    scores = reduced_backward(scores)
    allowed = (key_pos[None, :] <= query_pos[:, None])[:, None, None, :]
    masked = jnp.where(allowed, scores, negative_filler)
    highest = lax.optimization_barrier(jnp.max(masked, axis=-1, keepdims=True))
    expval = jnp.exp(masked - highest)
    probs = expval / lax.optimization_barrier(jnp.sum(expval, axis=-1, keepdims=True))
    mixed = jnp.einsum('qkgs,skd->qkgd', reduced_input(probs), value_head_rows, precision=lax.Precision.HIGHEST)
    return mixed.reshape(local_rows, QUERY_HEADS * HEAD_SIZE)

def attention(query_rows, key_head_rows, value_head_rows, token_positions):
    block_rows = min(512, SEQUENCE_TOKENS)
    block_count = SEQUENCE_TOKENS // block_rows

    def one_block(block_pair):
        return attend_block(block_pair[0], key_head_rows, value_head_rows, block_pair[1], token_positions)
    mixed = lax.map(jax.checkpoint(one_block), (query_rows.reshape(block_count, block_rows, QUERY_HEADS, HEAD_SIZE), token_positions.reshape(block_count, block_rows)))
    return mixed.reshape(SEQUENCE_TOKENS, QUERY_HEADS * HEAD_SIZE)

def layer(layer_in, token_positions, params):
    gain_one, query_proj, key_projection, value_projection, out_proj, gain_two, gate_proj, up_proj, down_proj = params
    normalized_input = reduced_input(rms_norm(layer_in, gain_one))
    query_rows = reduced_input(rotary_embed(reduced_backward(matrix_product_exact(normalized_input, query_proj)).reshape(SEQUENCE_TOKENS, QUERY_HEADS, HEAD_SIZE), token_positions))
    key_head_rows = reduced_input(rotary_embed(reduced_backward(matrix_product_exact(normalized_input, key_projection)).reshape(SEQUENCE_TOKENS, KEY_VALUE_HEADS, HEAD_SIZE), token_positions))
    value_head_rows = reduced_input(reduced_backward(matrix_product_exact(normalized_input, value_projection)).reshape(SEQUENCE_TOKENS, KEY_VALUE_HEADS, HEAD_SIZE))
    attended = reduced_input(reduced_backward(attention(query_rows, key_head_rows, value_head_rows, token_positions)))
    hidden = layer_in + reduced_backward(matrix_product_exact(attended, out_proj))
    normed_mid = reduced_input(rms_norm(hidden, gain_two))
    gate_val = reduced_backward(matrix_product_exact(normed_mid, gate_proj))
    up_val = reduced_backward(matrix_product_exact(normed_mid, up_proj))
    inner_low = reduced_input(gate_val * jax.nn.sigmoid(gate_val) * up_val)
    return hidden + reduced_backward(matrix_product_exact(inner_low, down_proj))

def reference(inputs, piece_order, cotangent, gain_attn, w_query, key_weight, value_weight, w_out, gain_mlp, w_gate, w_up, w_down):
    params = tuple((tensor.astype(jnp.float32) for tensor in (gain_attn, w_query, key_weight, value_weight, w_out, gain_mlp, w_gate, w_up, w_down)))
    seq_total = MICRO * SEQS
    flat_in = inputs.astype(jnp.float32).reshape(seq_total, SEQUENCE_TOKENS, MODEL_DIMENSION)
    flat_cot = cotangent.astype(jnp.float32).reshape(seq_total, SEQUENCE_TOKENS, MODEL_DIMENSION)
    flat_order = piece_order.astype(jnp.int32).reshape(seq_total, SEQUENCE_TOKENS // PIECE)
    token_positions = (flat_order[:, :, None] * PIECE + jnp.arange(PIECE, dtype=jnp.int32)[None, None, :]).reshape(seq_total, SEQUENCE_TOKENS).astype(jnp.int32)
    offsets = jnp.zeros_like(flat_in)

    def whole_model(start_in, offset_in, weights):
        first_section = tuple((tensor[0] for tensor in weights))
        second_section = tuple((tensor[1] for tensor in weights))

        def one_sequence(carry_val, item_set):
            seq_in, seq_pos, seq_offset = item_set
            early = layer(seq_in, seq_pos, first_section)
            late = layer(reduced_backward(reduced_input(early) + seq_offset), seq_pos, second_section)
            return (carry_val, (early, late))
        unused, outs_pair = lax.scan(jax.checkpoint(one_sequence), jnp.zeros((), jnp.float32), (start_in, token_positions, offset_in))
        return outs_pair
    (early_all, late_all), pullback = jax.vjp(whole_model, flat_in, offsets, params)
    grad_in, grad_offset, grad_params = pullback((jnp.zeros_like(early_all), flat_cot))
    acts = jnp.stack([early_all, late_all]).reshape(2, MICRO, SEQS, SEQUENCE_TOKENS, MODEL_DIMENSION).astype(jnp.bfloat16)
    input_grads = jnp.stack([grad_in, grad_offset]).reshape(2, MICRO, SEQS, SEQUENCE_TOKENS, MODEL_DIMENSION).astype(jnp.bfloat16)
    return (acts, input_grads, grad_params[0], grad_params[1], grad_params[2], grad_params[3], grad_params[4], grad_params[5], grad_params[6], grad_params[7], grad_params[8])
```

```python
import functools

import jax
import jax.numpy as jnp
from jax import lax
from jax.experimental import pallas as pl
from jax.experimental.pallas import tpu as pltpu
from jax.sharding import PartitionSpec as P

D = 576
HEADS = 9
KVH = 3
HD = 64
FF = 1536
ROWS = 64
TOK = 128
EPS = 1e-05
ROPE_BASE = 100000.0
FILL = -1e30
BF = jnp.bfloat16
F32 = jnp.float32
MESH = pl.DeviceIdType.MESH
VMEM = pltpu.VMEM
VLIM = 56 * 2**20


def mm(a, b):
    return jnp.dot(a, b, preferred_element_type=F32)


def mmt(a, b):
    return lax.dot_general(a, b, (((1,), (1,)), ((), ())), preferred_element_type=F32)


def tmm(a, b):
    return lax.dot_general(a, b, (((0,), (0,)), ((), ())), preferred_element_type=F32)


def place():
    c = lax.axis_index("ctx")
    return lax.axis_index("section"), c // 4, c % 4, lax.axis_index("fsdp")


def xp(x, y, d):
    return {"ctx": lax.rem(x + d, 4) * 4 + y}


def yp(x, y, d):
    return {"ctx": x * 4 + lax.rem(y + d, 4)}


def zp(z, d):
    return {"fsdp": lax.rem(z + d, 4)}


def greet(peers):
    barrier = pltpu.get_barrier_semaphore()
    for peer in peers:
        pl.semaphore_signal(barrier, inc=1, device_id=peer, device_id_type=MESH)
    pl.semaphore_wait(barrier, len(peers))


class Copies:
    def __init__(self, send, recv):
        self.send, self.recv, self.n = send, recv, 0
        self.all = []

    def push(self, src, dst, peer):
        i = self.n
        self.n += 1
        cp = pltpu.make_async_remote_copy(
            src_ref=src,
            dst_ref=dst,
            send_sem=self.send.at[i],
            recv_sem=self.recv.at[i],
            device_id=peer,
            device_id_type=MESH,
        )
        cp.start()
        self.all.append(cp)
        return cp

    def finish(self):
        for cp in self.all:
            cp.wait_send()


def xy_peers(x, y):
    return [xp(x, y, d) for d in (1, 2, 3)] + [yp(x, y, d) for d in (1, 2, 3)]


def weights_kernel(shard, w, send, recv, local):
    s, x, y, z = place()
    sib = {"section": 1 - s}
    greet(xy_peers(x, y) + [zp(z, d) for d in (1, 2, 3)] + [sib])
    cps = Copies(send, recv)
    zrows = pl.ds(pl.multiple_of(144 * z, 16), 144)
    own = pltpu.make_async_copy(shard.at[x, y], w.at[s, x, y, zrows], local)
    own.start()
    got = [
        cps.push(shard.at[x, y], w.at[s, x, y, zrows], zp(z, d)) for d in (1, 2, 3)
    ]
    own.wait()
    for cp in got:
        cp.wait_recv()
    ra, rb = pl.ds(0, 288), pl.ds(288, 288)
    got = []
    for d in (1, 2, 3):
        got.append(cps.push(w.at[s, x, y, ra], w.at[s, x, y, ra], xp(x, y, d)))
        got.append(cps.push(w.at[s, x, y, rb], w.at[s, x, y, rb], yp(x, y, d)))
    for cp in got:
        cp.wait_recv()
    got = []
    for d in (1, 2, 3):
        got.append(cps.push(w.at[s, :, y, ra], w.at[s, :, y, ra], yp(x, y, d)))
        got.append(cps.push(w.at[s, x, :, rb], w.at[s, x, :, rb], xp(x, y, d)))
    last = [
        cps.push(w.at[s, :, y, ra], w.at[s, :, y, ra], sib),
        cps.push(w.at[s, x, :, rb], w.at[s, x, :, rb], sib),
    ]
    for i, d in enumerate((1, 2, 3)):
        got[2 * i].wait_recv()
        fy = lax.rem(y + 4 - d, 4)
        last.append(cps.push(w.at[s, :, fy, ra], w.at[s, :, fy, ra], sib))
        got[2 * i + 1].wait_recv()
        fx = lax.rem(x + 4 - d, 4)
        last.append(cps.push(w.at[s, fx, :, rb], w.at[s, fx, :, rb], sib))
    for cp in last:
        cp.wait_recv()
    cps.finish()


def gather_weights(shard):
    n = 3 + 6 + 6 + 8
    return pl.pallas_call(
        weights_kernel,
        name="weights",
        out_shape=jax.ShapeDtypeStruct((2, 4, 4, D, 384), BF),
        in_specs=[pl.BlockSpec(memory_space=pl.ANY)],
        out_specs=pl.BlockSpec(memory_space=pl.ANY),
        scratch_shapes=[
            pltpu.SemaphoreType.DMA((n,)),
            pltpu.SemaphoreType.DMA((n,)),
            pltpu.SemaphoreType.DMA,
        ],
        compiler_params=pltpu.CompilerParams(collective_id=0, has_side_effects=True),
    )(shard)


def rope(v, cos, sin):
    lane = lax.broadcasted_iota(jnp.int32, v.shape, 1)
    turned = jnp.where(lane % 64 < 32, pltpu.roll(v, 96, 1), pltpu.roll(v, 32, 1))
    return v * cos + turned * sin


def kv_tables(cos, sin):
    lane = lax.broadcasted_iota(jnp.int32, cos.shape, 1)
    return jnp.where(lane < 64, cos, 1.0), jnp.where(lane < 64, sin, 0.0)


def low_lanes(v):
    lane = lax.broadcasted_iota(jnp.int32, v.shape, 1)
    return jnp.where(lane < 64, v, jnp.zeros_like(v))


def high_lanes(v):
    lane = lax.broadcasted_iota(jnp.int32, v.shape, 1)
    return jnp.where(lane < 64, jnp.zeros_like(v), v)


def inv_rms(v):
    return lax.rsqrt(jnp.mean(v * v, axis=-1, keepdims=True) + EPS)


def qkv_kernel(
    x_ref, gain_ref, w_ref, cos_ref, sin_ref, n1_ref, q_ref, kv_ref, send, recv
):
    s, x, y, z = place()
    v = x_ref[...].astype(F32)
    n1 = (v * inv_rms(v) * gain_ref[...]).astype(BF)
    n1_ref[...] = n1
    cos, sin = cos_ref[...], sin_ref[...]
    ckv, skv = kv_tables(cos, sin)
    kv = mm(n1, w_ref[3])
    for j in range(KVH):
        blk = rope(kv[:, 128 * j : 128 * j + 128], ckv, skv).astype(BF)
        for m in range(2):
            kv_ref[m, x, y, :, 128 * j : 128 * j + 128] = blk[64 * m : 64 * m + 64]
    greet(xy_peers(x, y))
    cps = Copies(send, recv)
    got = []
    for d in (1, 2, 3):
        got.append(cps.push(kv_ref.at[0, x, y], kv_ref.at[0, x, y], xp(x, y, d)))
        got.append(cps.push(kv_ref.at[1, x, y], kv_ref.at[1, x, y], yp(x, y, d)))
    qq = [mm(n1, w_ref[0]), mm(n1, w_ref[1][:, :256])]
    q = jnp.concatenate(qq, axis=1) * 0.125
    for b in range(5):
        blk = rope(q[:, 128 * b : 128 * b + 128], cos, sin)
        for half in range(2):
            h = 2 * b + half
            if h >= HEADS:
                continue
            part = low_lanes(blk if half == 0 else pltpu.roll(blk, 64, 1)).astype(BF)
            j, g = h // 3, h % 3
            for m in range(2):
                q_ref[3 * m + j, 64 * g : 64 * g + 64] = part[64 * m : 64 * m + 64]
    for cp in got:
        cp.wait_recv()
    got = []
    for d in (1, 2, 3):
        got.append(cps.push(kv_ref.at[0, :, y], kv_ref.at[0, :, y], yp(x, y, d)))
        got.append(cps.push(kv_ref.at[1, x], kv_ref.at[1, x], xp(x, y, d)))
    for cp in got:
        cp.wait_recv()
    cps.finish()


def vm():
    return pl.BlockSpec(memory_space=pltpu.VMEM)


def hbm():
    return pl.BlockSpec(memory_space=pl.ANY)


def qkv_call(layer, xin, gain, w, cos, sin):
    return pl.pallas_call(
        qkv_kernel,
        name="qkv",
        grid=(1,),
        out_shape=(
            jax.ShapeDtypeStruct((TOK, D), BF),
            jax.ShapeDtypeStruct((6, 192, 128), BF),
            jax.ShapeDtypeStruct((2, 4, 4, ROWS, 384), BF),
        ),
        in_specs=[
            vm(),
            vm(),
            pl.BlockSpec((None, 4, D, 384), lambda i: (layer, 0, 0, 0)),
            vm(),
            vm(),
        ],
        out_specs=(vm(), vm(), vm()),
        scratch_shapes=[
            pltpu.SemaphoreType.DMA((12,)),
            pltpu.SemaphoreType.DMA((12,)),
        ],
        compiler_params=pltpu.CompilerParams(
            collective_id=1 + layer, has_side_effects=True, vmem_limit_bytes=VLIM
        ),
    )(xin, gain, w, cos, sin)


def fwd_kernel(
    x_ref, q_ref, kv_ref, qpos_ref, kpos_ref, gain_ref, w_hbm,
    act_ref, h_ref, o_ref, p_ref, g_ref, u_ref, m_ref,
    w_ref, sem,
):
    layer = sem[1]
    loads = [
        pltpu.make_async_copy(w_hbm.at[layer, 1 + 0], w_ref.at[0], sem[0].at[0]),
        pltpu.make_async_copy(w_hbm.at[layer, 2], w_ref.at[1], sem[0].at[1]),
        pltpu.make_async_copy(
            w_hbm.at[layer, pl.ds(4, 12)], w_ref.at[pl.ds(2, 12)], sem[0].at[2]
        ),
    ]
    for cp in loads:
        cp.start()
    heads = {}
    for m in range(2):
        allowed = kpos_ref[m : m + 1, :] <= qpos_ref[m]
        for j in range(KVH):
            kvb = kv_ref[m, :, 128 * j : 128 * j + 128]
            sc = jnp.where(allowed, mmt(q_ref[3 * m + j], kvb), FILL)
            e = jnp.exp(sc - jnp.max(sc, axis=-1, keepdims=True))
            p = (e * (1.0 / jnp.sum(e, axis=-1, keepdims=True))).astype(BF)
            p_ref[3 * m + j] = p
            o = mm(p, kvb)
            for g in range(3):
                heads[m, 3 * j + g] = o[64 * g : 64 * g + 64]
        for b in range(5):
            hi = high_lanes(heads[m, 2 * b])
            if b > 0:
                hi = hi + low_lanes(pltpu.roll(heads[m, 2 * b - 1], 64, 1))
            o_ref[64 * m : 64 * m + 64, 128 * b : 128 * b + 128] = hi.astype(BF)
    for cp in loads:
        cp.wait()
    ob = o_ref[...]
    h = x_ref[...].astype(F32) + (
        mmt(ob[:, :256], w_ref[0][:, 128:384]) + mmt(ob[:, 256:], w_ref[1])
    )
    h_ref[...] = h
    n2 = (h * inv_rms(h) * gain_ref[...]).astype(BF)
    acc = h
    for i in range(4):
        cols = slice(384 * i, 384 * i + 384)
        g = mm(n2, w_ref[2 + i])
        u = mm(n2, w_ref[6 + i])
        g_ref[:, cols] = g
        u_ref[:, cols] = u
        low = (g * jax.nn.sigmoid(g) * u).astype(BF)
        m_ref[:, cols] = low
        acc = acc + mmt(low, w_ref[10 + i])
    act_ref[...] = acc.astype(BF)


def fwd_call(layer, xin, q, kv, qpos, kpos, gain, w):
    def kernel(*refs):
        fwd_kernel(*refs[:-1], (refs[-1], layer))

    return pl.pallas_call(
        kernel,
        name="forward",
        out_shape=(
            jax.ShapeDtypeStruct((TOK, D), BF),
            jax.ShapeDtypeStruct((TOK, D), F32),
            jax.ShapeDtypeStruct((TOK, 640), BF),
            jax.ShapeDtypeStruct((6, 192, 1024), BF),
            jax.ShapeDtypeStruct((TOK, FF), F32),
            jax.ShapeDtypeStruct((TOK, FF), F32),
            jax.ShapeDtypeStruct((TOK, FF), BF),
        ),
        in_specs=[vm()] * 6 + [hbm()],
        out_specs=(vm(),) * 7,
        scratch_shapes=[VMEM((14, D, 384), BF), pltpu.SemaphoreType.DMA((3,))],
        compiler_params=pltpu.CompilerParams(vmem_limit_bytes=VLIM),
    )(xin, q, kv, qpos, kpos, gain, w)


def bwd_kernel(
    layer, dy_ref, h_ref, p_ref, g_ref, u_ref, m_ref, q_ref, kv_ref, gain_ref,
    cos_ref, sin_ref, w_hbm, *rest,
):
    dh_ref, dq_ref, dkv_ref, gg_ref, grads, w_ref, gbuf, wsem, gsem = rest[-9:]
    loads = [
        pltpu.make_async_copy(
            w_hbm.at[layer, pl.ds(4, 12)], w_ref.at[pl.ds(2, 12)], wsem.at[2]
        ),
        pltpu.make_async_copy(w_hbm.at[layer, pl.ds(1, 2)], w_ref.at[pl.ds(0, 2)], wsem.at[0]),
    ]
    for cp in loads:
        cp.start()
    dyb = dy_ref[...]
    h = h_ref[...]
    r = inv_rms(h)
    gain = gain_ref[...]
    n2 = (h * r * gain).astype(BF)
    dyt = dyb.T
    n2t = n2.T
    loads[0].wait()
    dn2 = jnp.zeros((TOK, D), F32)
    outs = []
    for i in range(4):
        cols = slice(384 * i, 384 * i + 384)
        dm = mm(dyb, w_ref[10 + i])
        g = g_ref[:, cols]
        u = u_ref[:, cols]
        sg = jax.nn.sigmoid(g)
        dg = (dm * u * sg * (1.0 + g * (1.0 - sg))).astype(BF)
        du = (dm * g * sg).astype(BF)
        gbuf[0, i] = mm(n2t, dg).astype(BF)
        gbuf[1, i] = mm(n2t, du).astype(BF)
        gbuf[2, i] = mm(dyt, m_ref[:, cols]).astype(BF)
        for k in range(3):
            cp = pltpu.make_async_copy(
                gbuf.at[k, i], grads.at[layer, 1 + k, i], gsem.at[3 * i + k]
            )
            cp.start()
            outs.append(cp)
        dn2 = dn2 + mmt(dg, w_ref[2 + i]) + mmt(du, w_ref[6 + i])
    scaled = dn2 * gain
    inner = jnp.mean(scaled * h, axis=-1, keepdims=True)
    dh = dyb.astype(F32) + (r * scaled - h * (r * r * r) * inner)
    gg_ref[...] = jnp.sum(dn2 * h * r, axis=0, keepdims=True)
    dh_ref[...] = dh
    dhb = dh.astype(BF)
    loads[1].wait()
    do = jnp.concatenate([mm(dhb, w_ref[0][:, 128:384]), mm(dhb, w_ref[1])], axis=1)
    dqs = {}
    for m in range(2):
        for j in range(KVH):
            kvb = kv_ref[m, :, 128 * j : 128 * j + 128]
            parts = []
            for g in range(3):
                hh = 3 * j + g
                b = (hh + 1) // 2
                blk = do[64 * m : 64 * m + 64, 128 * b : 128 * b + 128]
                parts.append(
                    high_lanes(blk if hh % 2 == 0 else pltpu.roll(blk, 64, 1))
                )
            dop = jnp.concatenate(parts, axis=0).astype(BF)
            pb = p_ref[3 * m + j]
            p = pb.astype(F32)
            dp = mmt(dop, kvb)
            delta = jnp.sum(p * dp, axis=-1, keepdims=True)
            ds = (p * (dp - delta)).astype(BF)
            dq = mm(ds, kvb) * 0.125
            for g in range(3):
                dqs[m, 3 * j + g] = dq[64 * g : 64 * g + 64]
            dkvt = mm(q_ref[3 * m + j].T, ds) + mm(dop.T, pb)
            dkv_ref[m, :, 128 * j : 128 * j + 128] = dkvt.T.astype(BF)
        cos, sin = cos_ref[64 * m : 64 * m + 64], sin_ref[64 * m : 64 * m + 64]
        for b in range(5):
            blk = low_lanes(dqs[m, 2 * b])
            if 2 * b + 1 < HEADS:
                blk = blk + high_lanes(pltpu.roll(dqs[m, 2 * b + 1], 64, 1))
            dq_ref[64 * m : 64 * m + 64, 128 * b : 128 * b + 128] = rope(
                blk, cos, -sin
            ).astype(BF)
    for cp in outs:
        cp.wait()


def bwd_call(layer, dy, h, p, g, u, m, q, kv, gain, cos, sin, w, grads):
    started = [] if grads is None else [grads]
    return pl.pallas_call(
        functools.partial(bwd_kernel, layer),
        name="backward",
        out_shape=(
            jax.ShapeDtypeStruct((TOK, D), F32),
            jax.ShapeDtypeStruct((TOK, 640), BF),
            jax.ShapeDtypeStruct((2, 1024, 384), BF),
            jax.ShapeDtypeStruct((1, D), F32),
            jax.ShapeDtypeStruct((2, 4, 4, D, 384), BF),
        ),
        in_specs=[vm()] * 11 + [hbm()] * (1 + len(started)),
        out_specs=(vm(), vm(), vm(), vm(), hbm()),
        scratch_shapes=[
            VMEM((14, D, 384), BF),
            VMEM((3, 4, D, 384), BF),
            pltpu.SemaphoreType.DMA((3,)),
            pltpu.SemaphoreType.DMA((12,)),
        ],
        input_output_aliases={12: 4} if started else {},
        compiler_params=pltpu.CompilerParams(vmem_limit_bytes=VLIM),
    )(dy, h, p, g, u, m, q, kv, gain, cos, sin, w, *started)


def dkv_kernel(
    layer, part_ref, n1_ref, dq_ref, o_ref, dh_ref, x_ref, gain_ref, w_ref,
    cos_ref, sin_ref, grads_in,
    dx_ref, gg_ref, grads,
    got1, got2, mid, gbuf, send, recv, gsem,
):
    s, x, y, z = place()
    greet(xy_peers(x, y))
    cps = Copies(send, recv)
    one = []
    for d in (1, 2, 3):
        ty, tx = lax.rem(y + d, 4), lax.rem(x + d, 4)
        one.append(cps.push(part_ref.at[0, :, ty], got1.at[0, d - 1], yp(x, y, d)))
        one.append(cps.push(part_ref.at[1, tx], got1.at[1, d - 1], xp(x, y, d)))
    n1 = n1_ref[...]
    dqb = dq_ref[...]
    dh = dh_ref[...]
    ob = o_ref[...]
    zero = jnp.zeros((TOK, 512), BF)
    left = jnp.concatenate([n1, dh.astype(BF)], axis=0).T
    right = jnp.concatenate(
        [jnp.concatenate([dqb, zero], axis=1), jnp.concatenate([zero, ob], axis=1)],
        axis=0,
    )
    outs = []
    for i in range(3):
        gbuf[i] = mm(left, right[:, 384 * i : 384 * i + 384]).astype(BF)
        cp = pltpu.make_async_copy(gbuf.at[i], grads.at[layer, 0, i], gsem.at[i])
        cp.start()
        outs.append(cp)
    dn1 = mmt(dqb[:, :384], w_ref[0]) + mmt(dqb[:, 384:], w_ref[1][:, :256])
    for cp in one:
        cp.wait_recv()
    for i in range(4):
        a = part_ref[0, i, y].astype(F32)
        b = part_ref[1, x, i].astype(F32)
        for d in range(3):
            a = a + got1[0, d, i].astype(F32)
            b = b + got1[1, d, i].astype(F32)
        mid[0, i] = a.astype(BF)
        mid[1, i] = b.astype(BF)
    two = []
    for d in (1, 2, 3):
        ty, tx = lax.rem(y + d, 4), lax.rem(x + d, 4)
        two.append(cps.push(mid.at[0, tx], got2.at[0, d - 1], xp(x, y, d)))
        two.append(cps.push(mid.at[1, ty], got2.at[1, d - 1], yp(x, y, d)))
    for cp in two:
        cp.wait_recv()
    a = mid[0, x].astype(F32)
    b = mid[1, y].astype(F32)
    for d in range(3):
        a = a + got2[0, d].astype(F32)
        b = b + got2[1, d].astype(F32)
    total = jnp.concatenate([a, b], axis=0)
    ckv, skv = kv_tables(cos_ref[...], -sin_ref[...])
    dkv = jnp.concatenate(
        [rope(total[:, 128 * j : 128 * j + 128], ckv, skv) for j in range(KVH)], axis=1
    ).astype(BF)
    gbuf[3] = tmm(n1, dkv).astype(BF)
    cp = pltpu.make_async_copy(gbuf.at[3], grads.at[layer, 0, 3], gsem.at[3])
    cp.start()
    outs.append(cp)
    dn1 = dn1 + mmt(dkv, w_ref[3])
    v = x_ref[...].astype(F32)
    r = inv_rms(v)
    scaled = dn1 * gain_ref[...]
    inner = jnp.mean(scaled * v, axis=-1, keepdims=True)
    dx_ref[...] = (dh + (r * scaled - v * (r * r * r) * inner)).astype(BF)
    gg_ref[...] = jnp.sum(dn1 * v * r, axis=0, keepdims=True)
    for cp in outs:
        cp.wait()
    cps.finish()


def dkv_call(layer, part, n1, dq, o, dh, xin, gain, w, cos, sin, grads):
    return pl.pallas_call(
        functools.partial(dkv_kernel, layer),
        name="dkv",
        grid=(1,),
        out_shape=(
            jax.ShapeDtypeStruct((TOK, D), BF),
            jax.ShapeDtypeStruct((1, D), F32),
            jax.ShapeDtypeStruct(grads.shape, BF),
        ),
        in_specs=[vm()] * 7
        + [pl.BlockSpec((None, 4, D, 384), lambda i: (layer, 0, 0, 0))]
        + [vm()] * 2
        + [hbm()],
        out_specs=(vm(), vm(), hbm()),
        scratch_shapes=[
            VMEM((2, 3, 4, ROWS, 384), BF),
            VMEM((2, 3, ROWS, 384), BF),
            VMEM((2, 4, ROWS, 384), BF),
            VMEM((4, D, 384), BF),
            pltpu.SemaphoreType.DMA((12,)),
            pltpu.SemaphoreType.DMA((12,)),
            pltpu.SemaphoreType.DMA((4,)),
        ],
        input_output_aliases={10: 2},
        compiler_params=pltpu.CompilerParams(
            collective_id=3 + layer, has_side_effects=True, vmem_limit_bytes=VLIM
        ),
    )(part, n1, dq, o, dh, xin, gain, w, cos, sin, grads)


def add_into(dst, srcs, chunk=96):
    rows = dst.shape[0]

    def step(i, carry):
        at = pl.ds(pl.multiple_of(i * chunk, 16), chunk)
        total = dst[at].astype(F32)
        for src in srcs:
            total = total + src[at].astype(F32)
        dst[at] = total.astype(BF)
        return carry

    lax.fori_loop(0, rows // chunk, step, 0)


def reduce_kernel(
    grads, gains, pairs, out, gout, pout,
    hold, sib_in, ra_in, rb_in, r2a, r2b, fin, r3, gsum, gin, send, recv, lsem,
):
    s, x, y, z = place()
    sib = {"section": 1 - s}
    peers = xy_peers(x, y) + [zp(z, d) for d in (1, 2, 3)] + [sib]
    greet(peers)
    cps = Copies(send, recv)
    ra, rb = pl.ds(0, 288), pl.ds(288, 288)
    own = pltpu.make_async_copy(grads.at[s], hold, lsem.at[0])
    own.start()
    mine = pltpu.make_async_copy(gains.at[s], gsum, lsem.at[1])
    mine.start()
    half = [
        cps.push(grads.at[1 - s, i], sib_in.at[i], sib) for i in range(4)
    ]
    gcp = cps.push(gains.at[1 - s], gin.at[9], sib)
    pcp = cps.push(pairs.at[1 - s], pout, sib)
    own.wait()
    mine.wait()
    for i in range(4):
        half[i].wait_recv()
        for k in range(4):
            add_into(hold.at[i, k], [sib_in.at[i, k]])
    gcp.wait_recv()
    gsum[...] = gsum[...] + gin[9]
    one, gone = [], []
    for d in (1, 2, 3):
        tx, ty = lax.rem(x + d, 4), lax.rem(y + d, 4)
        one.append(cps.push(hold.at[tx, :, ra], ra_in.at[d - 1], xp(x, y, d)))
        one.append(cps.push(hold.at[:, ty, rb], rb_in.at[d - 1], yp(x, y, d)))
        gone.append(cps.push(gsum, gin.at[d - 1], xp(x, y, d)))
    for cp in one + gone:
        cp.wait_recv()
    for cp in gone:
        cp.wait_send()
        cps.all = [other for other in cps.all if other is not cp]
    for k in range(4):
        add_into(hold.at[x, k, ra], [ra_in.at[d, k] for d in range(3)])
        add_into(hold.at[k, y, rb], [rb_in.at[d, k] for d in range(3)])
    gsum[...] = gsum[...] + gin[0] + gin[1] + gin[2]
    two, gone = [], []
    for d in (1, 2, 3):
        tx, ty = lax.rem(x + d, 4), lax.rem(y + d, 4)
        two.append(cps.push(hold.at[x, ty, ra], r2a.at[d - 1], yp(x, y, d)))
        two.append(cps.push(hold.at[tx, y, rb], r2b.at[d - 1], xp(x, y, d)))
        gone.append(cps.push(gsum, gin.at[2 + d], yp(x, y, d)))
    for cp in two + gone:
        cp.wait_recv()
    for cp in gone:
        cp.wait_send()
        cps.all = [other for other in cps.all if other is not cp]
    add_into(hold.at[x, y, ra], [r2a.at[d] for d in range(3)])
    add_into(hold.at[x, y, rb], [r2b.at[d] for d in range(3)])
    gsum[...] = gsum[...] + gin[3] + gin[4] + gin[5]
    three, gone = [], []
    for d in (1, 2, 3):
        tz = pl.ds(pl.multiple_of(lax.rem(z + d, 4) * 144, 16), 144)
        three.append(cps.push(hold.at[x, y, tz], r3.at[d - 1], zp(z, d)))
        gone.append(cps.push(gsum, gin.at[5 + d], zp(z, d)))
    for cp in three + gone:
        cp.wait_recv()
    gout[...] = gsum[...] + gin[6] + gin[7] + gin[8]
    mz = pl.ds(pl.multiple_of(z * 144, 16), 144)
    total = hold[x, y, mz].astype(F32)
    for d in range(3):
        total = total + r3[d].astype(F32)
    out[x, y] = total.astype(BF)
    qa, qb = pl.ds(0, 80), pl.ds(80, 64)
    four = []
    for d in (1, 2, 3):
        four.append(cps.push(out.at[x, y, qa], out.at[x, y, qa], xp(x, y, d)))
        four.append(cps.push(out.at[x, y, qb], out.at[x, y, qb], yp(x, y, d)))
    for cp in four:
        cp.wait_recv()
    five = []
    for d in (1, 2, 3):
        five.append(cps.push(out.at[:, y, qa], out.at[:, y, qa], yp(x, y, d)))
        five.append(cps.push(out.at[x, :, qb], out.at[x, :, qb], xp(x, y, d)))
    for cp in five + [pcp]:
        cp.wait_recv()
    cps.finish()


def reduce_call(grads, gains, pairs):
    n = 6 + 9 + 9 + 6 + 6 + 6
    return pl.pallas_call(
        reduce_kernel,
        name="reduce",
        out_shape=(
            jax.ShapeDtypeStruct((4, 4, 144, 384), BF),
            jax.ShapeDtypeStruct((8, D), F32),
            jax.ShapeDtypeStruct((2, TOK, D), BF),
        ),
        in_specs=[hbm(), vm(), vm()],
        out_specs=(vm(), vm(), vm()),
        scratch_shapes=[
            VMEM((4, 4, D, 384), BF),
            VMEM((4, 4, D, 384), BF),
            VMEM((3, 4, 288, 384), BF),
            VMEM((3, 4, 288, 384), BF),
            VMEM((3, 288, 384), BF),
            VMEM((3, 288, 384), BF),
            VMEM((144, 384), BF),
            VMEM((3, 144, 384), BF),
            VMEM((8, D), F32),
            VMEM((10, 8, D), F32),
            pltpu.SemaphoreType.DMA((n,)),
            pltpu.SemaphoreType.DMA((n,)),
            pltpu.SemaphoreType.DMA((2,)),
        ],
        compiler_params=pltpu.CompilerParams(
            collective_id=5, has_side_effects=True, vmem_limit_bytes=VLIM
        ),
    )(grads, gains, pairs)


def pack(w_query, key_weight, value_weight, w_out, w_gate, w_up, w_down):
    kv = jnp.concatenate(
        [key_weight.reshape(144, 3, 64), value_weight.reshape(144, 3, 64)], axis=2
    ).reshape(144, 384)
    flat = jnp.concatenate([w_query, w_out.T, kv, w_gate, w_up, w_down.T], axis=1)
    return flat.reshape(144, 16, 384).transpose(1, 0, 2).reshape(4, 4, 144, 384)


def body(
    inputs, piece_order, cotangent, gain_attn, w_query, key_weight, value_weight,
    w_out, gain_mlp, w_gate, w_up, w_down,
):
    s = lax.axis_index("section")
    c = lax.axis_index("ctx")
    z = lax.axis_index("fsdp")
    shard = pack(
        w_query[0], key_weight[0], value_weight[0], w_out[0], w_gate[0], w_up[0], w_down[0]
    )
    w5 = gather_weights(shard)
    w = w5.reshape(2, 16, D, 384)
    gains = lax.all_gather(
        jnp.concatenate([gain_attn, gain_mlp], axis=0), ("section", "fsdp"), axis=0
    )
    gains = gains.reshape(2, 4, 2, 144).transpose(0, 2, 1, 3).reshape(2, 2, 1, D)
    gains = gains.astype(F32)

    order = lax.dynamic_slice_in_dim(piece_order[:, 0], 2 * s, 2, 0)
    kpos = (order[:, :, None] * 32 + jnp.arange(32, dtype=jnp.int32)).reshape(2, 1024)
    lpos = lax.dynamic_slice_in_dim(kpos, c * ROWS, ROWS, 1)
    qpos = jnp.tile(lpos, (1, 3)).reshape(2, 192, 1)
    frequency = ROPE_BASE ** (-jnp.arange(32, dtype=F32) / 32)
    angles = lpos.reshape(TOK, 1).astype(F32) * frequency[None, :]
    cos1, sin1 = jnp.cos(angles), jnp.sin(angles)
    cos = jnp.concatenate([cos1] * 4, axis=1)
    sin = jnp.concatenate([-sin1, sin1, -sin1, sin1], axis=1)

    x1 = lax.dynamic_slice_in_dim(inputs[:, 0], 2 * s, 2, 0).reshape(TOK, D)
    cot = lax.dynamic_slice_in_dim(cotangent[:, 0], 2 * s, 2, 0).reshape(TOK, D)

    xs, kept = [x1], []
    for layer in range(2):
        n1, q, kv = qkv_call(layer, xs[layer], gains[layer, 0], w, cos, sin)
        kv = kv.reshape(2, 1024, 384)
        act, h, o, p, g, u, m = fwd_call(
            layer, xs[layer], q, kv, qpos, kpos, gains[layer, 1], w
        )
        xs.append(act)
        kept.append((n1, q, kv, h, o, p, g, u, m))
    dy = cot
    grads = None
    dxs, ggs = [None, None], [None, None]
    for layer in (1, 0):
        n1, q, kv, h, o, p, g, u, m = kept[layer]
        dh, dq, dkv, gg2, grads = bwd_call(
            layer, dy, h, p, g, u, m, q, kv, gains[layer, 1], cos, sin, w, grads
        )
        dy, gg1, grads = dkv_call(
            layer, dkv.reshape(2, 4, 4, ROWS, 384), n1, dq, o, dh, xs[layer],
            gains[layer, 0], w, cos, sin, grads,
        )
        dxs[layer] = dy
        ggs[layer] = jnp.concatenate([gg1, gg2, jnp.zeros((6, D), F32)], axis=0)
    pairs = jnp.stack([jnp.stack([xs[l + 1], dxs[l]]) for l in range(2)])
    red, gsum, other = reduce_call(grads, jnp.stack(ggs), pairs)

    own = lax.dynamic_index_in_dim(pairs, s, 0, keepdims=False).reshape(2, 2, ROWS, D)
    other = other.reshape(2, 2, ROWS, D)
    first = s == 0
    both = jnp.concatenate(
        [jnp.where(first, own, other), jnp.where(first, other, own)], axis=1
    )
    flat = red.reshape(16, 144, 384).transpose(1, 0, 2).reshape(144, 6144).astype(F32)
    gsh = lax.dynamic_slice_in_dim(gsum, z * 144, 144, 1)
    kvg = flat[:, 1152:1536].reshape(144, 3, 2, 64)
    return (
        both[0][None, :, None],
        both[1][None, :, None],
        gsh[0:1],
        flat[None, :, 0:576],
        kvg[:, :, 0].reshape(1, 144, 192),
        kvg[:, :, 1].reshape(1, 144, 192),
        flat[:, 576:1152].T[None],
        gsh[1:2],
        flat[None, :, 1536:3072],
        flat[None, :, 3072:4608],
        flat[:, 4608:6144].T[None],
    )


def solution(mesh):
    placed = (
        P(None, "fsdp", "ctx", None),
        P(None, "fsdp", None),
        P(None, "fsdp", "ctx", None),
        P("section", "fsdp"),
        P("section", "fsdp", None),
        P("section", "fsdp", None),
        P("section", "fsdp", None),
        P("section", None, "fsdp"),
        P("section", "fsdp"),
        P("section", "fsdp", None),
        P("section", "fsdp", None),
        P("section", None, "fsdp"),
    )
    return jax.shard_map(
        body,
        mesh=mesh,
        in_specs=placed,
        out_specs=(
            P("section", None, "fsdp", "ctx", None),
            P("section", None, "fsdp", "ctx", None),
            P("section", "fsdp"),
            P("section", "fsdp", None),
            P("section", "fsdp", None),
            P("section", "fsdp", None),
            P("section", None, "fsdp"),
            P("section", "fsdp"),
            P("section", "fsdp", None),
            P("section", "fsdp", None),
            P("section", None, "fsdp"),
        ),
        check_vma=False,
    )
```
